32 devices in a mesh: row: 2 (over x), col: 4 (over y, core), layer: 4 (over z).
Axes of the slice: x: 2, y: 2, z: 4, core: 2. Of those that a mesh axis runs over, the one named last changes fastest.
Arguments:
- front: float32 [8192, 8192], P('row', ('col', 'layer')), may hold values from -8 to 256, as said below
Outputs:
- eliminated: float32 [8192, 8192], P('row', ('col', 'layer'))
The draws below stay inside these ranges and needn't reach their ends.
Inputs may be any that keep to these rules, and one draw needn't show every extreme that they name: `front`: every pivot block met during the elimination has a nonzero diagonal, and the Newton-Schulz iteration started from the inverse of its diagonal converges.
All inputs are finite; a program needn't handle non-finite values.
Results may differ from the reference program's by a relative error of at most 0.0001.
Values sent between devices are 32-bit elements; how exact they have to be, the bound alone decides.
A program may use at most 128 MiB of HBM per device.

```python
import jax
import jax.numpy as jnp
from jax import lax

M = 8192
B = 64
ITERS = 2
P_SIZE = 256


def draw_front(key, part):
    normal_key, diag_key = jax.random.split(jax.random.fold_in(key, 17), 2)
    scatter = jnp.clip(jax.random.normal(normal_key, (M, M), jnp.float32), -5.0, 5.0)
    leading = jax.random.uniform(diag_key, (M,), jnp.float32, 32.0, 64.0)
    places = jnp.arange(M)
    matrix = scatter.at[places, places].set(leading)
    return matrix


def setup_inputs(seed: int = 0) -> dict:
    seeds = jax.random.split(jax.random.key(seed), 2)
    return {
        "front": draw_front(jax.random.fold_in(seeds[1], 71), 0),
    }


def exact_dot(left, right):
    return jnp.dot(left, right, precision=lax.Precision.HIGHEST, preferred_element_type=jnp.float32)


def newton_inverse(pivot):
    inverse = jnp.diag(1.0 / jnp.diagonal(pivot))
    for sweep in range(ITERS):
        inverse = 2.0 * inverse - exact_dot(inverse, exact_dot(pivot, inverse))
    return inverse


def reference(front):
    matrix = front.astype(jnp.float32)
    for block in range(P_SIZE // B):
        block_begin = block * B
        block_end = block_begin + B
        pivot = matrix[block_begin:block_end, block_begin:block_end]
        inverse = newton_inverse(pivot)
        lower = exact_dot(matrix[block_end:, block_begin:block_end], inverse)
        upper = matrix[block_begin:block_end, block_end:]
        matrix = matrix.at[block_end:, block_end:].add(-exact_dot(lower, upper))
        matrix = matrix.at[block_end:, block_begin:block_end].set(lower)
    return matrix
```

```python
import functools

import jax
import jax.numpy as jnp
from jax import lax
from jax.experimental import pallas as pl
from jax.experimental.pallas import tpu as pltpu
from jax.sharding import PartitionSpec as P

B = 64
P_SIZE = 256
PIECE = 64
UNIT = 256
LEAD = 4
MESH = pl.DeviceIdType.MESH


def exact_dot(left, right):
    return jnp.dot(left, right, precision=lax.Precision.HIGHEST, preferred_element_type=jnp.float32)


def split(x):
    high = x.astype(jnp.bfloat16)
    low = (x - high.astype(jnp.float32)).astype(jnp.bfloat16)
    return high, low


def fused_dot(left, right):
    return jnp.dot(left, right, preferred_element_type=jnp.float32)


def kernel(
    layers, front, panel, out,
    held, share, rows_in, pivot, inner, x_buf, t_buf, g_high, g_low,
    recv_sem, rows_sem, load_sem, out_sem, send_sem,
):
    height, width = share.shape
    half = UNIT // 2
    pivot_pieces = P_SIZE // 2 // PIECE
    unit_pieces = half // PIECE
    units = height // UNIT
    total = pivot_pieces + units * unit_pieces
    order = list(range(pivot_pieces, pivot_pieces + LEAD)) + list(range(pivot_pieces))
    order += list(range(pivot_pieces + LEAD, total))

    r, col, z = lax.axis_index("row"), lax.axis_index("col"), lax.axis_index("layer")
    y, core = col // 2, col % 2
    flat = col * layers + z
    root_chip = jnp.logical_and(y == 0, z == 0)
    root = jnp.logical_and(root_chip, core == 0)
    has_sib = jnp.logical_not(jnp.logical_and(root_chip, core == 1))

    def device(row, yy, cc, zz):
        return (row, yy * 2 + cc, zz)

    along = jnp.logical_and(y == core, z < layers - 1)
    back = jnp.logical_and(jnp.logical_and(core == 0, y == 1), z == 1)
    has_one = jnp.logical_or(along, back)
    one = device(r, y, core, jnp.where(back, 0, jnp.minimum(z + 1, layers - 1)))
    has_two = jnp.logical_and(y == core, z >= 1)
    two = device(r, 1 - y, core, z)
    sib = device(r, y, 1 - core, z)
    tree_b = device(r, 1, 1, 0)
    other = device(1 - r, y, core, z)

    at_start = z == 0
    parent_y = jnp.where(at_start, jnp.where(core == 0, 1, 0), jnp.where(y == core, y, 1 - y))
    parent_z = jnp.where(at_start, jnp.where(core == 0, 1, 0), jnp.where(y == core, z - 1, z))
    parent_core = jnp.where(at_start, 0, core)
    barrier = pltpu.get_barrier_semaphore()

    @pl.when(jnp.logical_not(root_chip))
    def _():
        pl.semaphore_signal(
            barrier, inc=1, device_id=device(r, parent_y, parent_core, parent_z), device_id_type=MESH
        )

    @pl.when(jnp.logical_not(root))
    def _():
        pl.semaphore_signal(barrier, inc=1, device_id=sib, device_id_type=MESH)

    @pl.when(r == 1)
    def _():
        pl.semaphore_signal(barrier, inc=1, device_id=other, device_id_type=MESH)

    def row_of(t, i):
        return ((i - pivot_pieces) // unit_pieces) * UNIT + t * half + ((i - pivot_pieces) % unit_pieces) * PIECE

    @pl.when(root)
    def _():
        for i in order:
            for t in range(2):
                if i < pivot_pieces:
                    @pl.when(r == 0)
                    def _():
                        pltpu.make_async_copy(
                            panel.at[pl.ds(t * half + i * PIECE, PIECE), pl.ds(0, P_SIZE)],
                            held.at[t, pl.ds(i * PIECE, PIECE)],
                            recv_sem.at[t, i],
                        ).start()
                else:
                    pltpu.make_async_copy(
                        panel.at[pl.ds(row_of(t, i), PIECE), pl.ds(0, P_SIZE)],
                        held.at[t, pl.ds(i * PIECE, PIECE)],
                        recv_sem.at[t, i],
                    ).start()

    load = pltpu.make_async_copy(front, share, load_sem)
    load.start()

    @pl.when(r == 0)
    def _():
        pltpu.make_async_copy(front.at[pl.ds(0, P_SIZE)], rows_in, rows_sem).start()

    peers = (
        has_sib.astype(jnp.int32) + has_one.astype(jnp.int32) + has_two.astype(jnp.int32)
        + root.astype(jnp.int32) + (r == 0).astype(jnp.int32)
    )
    pl.when(peers > 0)(lambda: pl.semaphore_wait(barrier, peers))

    def piece(t, i, kind, target):
        return pltpu.make_async_remote_copy(
            src_ref=held.at[t, pl.ds(i * PIECE, PIECE)],
            dst_ref=held.at[t, pl.ds(i * PIECE, PIECE)],
            send_sem=send_sem.at[kind],
            recv_sem=recv_sem.at[t, i],
            device_id=target,
            device_id_type=MESH,
        )

    def arrived(t, i):
        pltpu.make_async_copy(
            held.at[t, pl.ds(i * PIECE, PIECE)], held.at[t, pl.ds(i * PIECE, PIECE)], recv_sem.at[t, i]
        ).wait()

    def forward(i):
        arrived(core, i)

        @pl.when(has_one)
        def _():
            piece(core, i, 0, one).start()

        @pl.when(has_two)
        def _():
            piece(core, i, 1, two).start()

        @pl.when(has_sib)
        def _():
            piece(core, i, 2, sib).start()

        @pl.when(root)
        def _():
            arrived(1, i)
            piece(1, i, 3, tree_b).start()
            piece(1, i, 4, sib).start()

    def pivot_piece_across(t, i):
        return pltpu.make_async_remote_copy(
            src_ref=panel.at[pl.ds(t * half + i * PIECE, PIECE), pl.ds(0, P_SIZE)],
            dst_ref=held.at[t, pl.ds(i * PIECE, PIECE)],
            send_sem=send_sem.at[5 + t],
            recv_sem=recv_sem.at[t, i],
            device_id=other,
            device_id_type=MESH,
        )

    @pl.when(jnp.logical_and(root, r == 0))
    def _():
        for i in range(pivot_pieces):
            for t in range(2):
                pivot_piece_across(t, i).start()

    def rows_across():
        return pltpu.make_async_remote_copy(
            src_ref=front.at[pl.ds(0, P_SIZE)],
            dst_ref=rows_in,
            send_sem=send_sem.at[7],
            recv_sem=rows_sem,
            device_id=other,
            device_id_type=MESH,
        )

    def other_arrived(i):
        @pl.when(jnp.logical_not(root))
        def _():
            arrived(1 - core, i)

    queue = list(order)

    def forward_some(count):
        for _ in range(min(count, len(queue))):
            forward(queue.pop(0))

    forward_some(LEAD + pivot_pieces)

    @pl.when(r == 0)
    def _():
        rows_across().start()

    for i in range(pivot_pieces):
        other_arrived(i)
    pivot[pl.ds(0, half), :] = held[0, pl.ds(0, half), :]
    pivot[pl.ds(half, half), :] = held[1, pl.ds(0, half), :]
    inner[...] = jnp.zeros_like(inner)

    eye = lax.broadcasted_iota(jnp.int32, (B, B), 0) == lax.broadcasted_iota(jnp.int32, (B, B), 1)
    blocks = P_SIZE // B
    for k in range(blocks):
        lo, hi = k * B, (k + 1) * B
        d = pivot[lo:hi, lo:hi]
        diagonal = jnp.where(eye, d, 0.0)
        down = 1.0 / jnp.sum(diagonal, axis=1, keepdims=True)
        across = 1.0 / jnp.sum(diagonal, axis=0, keepdims=True)
        x = jnp.where(eye, 2.0 * down, 0.0) - down * (d * across)
        x_buf[...] = x
        t_buf[...] = exact_dot(d, x)
        forward_some(1)
        x = x_buf[...]
        x = 2.0 * x - exact_dot(x, t_buf[...])
        x_buf[...] = x
        inner[lo:hi, lo:hi] = x
        forward_some(1)
        x = x_buf[...]
        if k < blocks - 1:
            pivot[hi:, lo:hi] = exact_dot(pivot[hi:, lo:hi], x)
            forward_some(1)
        if k > 0:
            inner[0:lo, lo:hi] = -exact_dot(exact_dot(inner[0:lo, 0:lo], pivot[0:lo, lo:hi]), x)
            forward_some(1)
        if k < blocks - 1:
            lower = pivot[hi:, lo:hi]
            pivot[hi:, hi:] = pivot[hi:, hi:] - exact_dot(lower, pivot[lo:hi, hi:])
            forward_some(1)
            if k == 0:
                pltpu.make_async_copy(rows_in, rows_in, rows_sem).wait()
            rows_in[hi:, :] = rows_in[hi:, :] - exact_dot(lower, rows_in[lo:hi, :])
            forward_some(1)

    owned = min(width, P_SIZE)
    g = exact_dot(inner[...], rows_in[...])
    high, low = split(g)
    g_high[...] = high
    g_low[...] = low
    for f in range(P_SIZE // owned):
        @pl.when(flat == f)
        def _():
            high, low = split(-inner[:, f * owned : (f + 1) * owned])
            g_high[:, 0:owned] = high
            g_low[:, 0:owned] = low
            rows_in[:, 0:owned] = pivot[:, f * owned : (f + 1) * owned]

    load.wait()
    kept = flat * width + lax.broadcasted_iota(jnp.int32, (half, width), 1) >= P_SIZE

    def update(u):
        for j in range(unit_pieces):
            other_arrived(pivot_pieces + u * unit_pieces + j)
        start = pivot_pieces * PIECE + u * half
        if not isinstance(u, int):
            start = pl.multiple_of(start, PIECE)
        for t in range(2):
            high, low = split(held[t, pl.ds(start, half), :])
            drop = fused_dot(high, g_high[...]) + fused_dot(high, g_low[...]) + fused_dot(low, g_high[...])
            place = pl.ds(u * UNIT + t * half, half)
            share[place, :] = jnp.where(kept, share[place, :], 0.0) - drop

        pltpu.make_async_copy(
            share.at[pl.ds(u * UNIT, UNIT)], out.at[pl.ds(u * UNIT, UNIT)], out_sem
        ).start()

    @pl.when(r == 0)
    def _():
        for j in range(unit_pieces):
            other_arrived(pivot_pieces + j)
        share[0:UNIT, :] = rows_in[...]
        pltpu.make_async_copy(share.at[pl.ds(0, UNIT)], out.at[pl.ds(0, UNIT)], out_sem).start()

    @pl.when(r != 0)
    def _():
        update(0)

    done = 1
    rest = len(queue)
    first = queue[0] if rest else 0

    def step(s, carry):
        forward(first + s)
        update(done + s)
        return carry

    beside = min(rest, units - 1)
    lax.fori_loop(0, beside, step, 0)
    if rest > beside:
        lax.fori_loop(first + beside, first + rest, lambda i, c: (forward(i), c)[1], 0)
    lax.fori_loop(done + beside, units, lambda u, c: (update(u), c)[1], 0)

    def sent(t, kind):
        pltpu.make_async_copy(held.at[t], held.at[t], send_sem.at[kind]).wait()

    pl.when(has_one)(lambda: sent(0, 0))
    pl.when(has_two)(lambda: sent(0, 1))
    pl.when(has_sib)(lambda: sent(0, 2))

    @pl.when(root)
    def _():
        sent(1, 3)
        sent(1, 4)

    @pl.when(jnp.logical_and(root, r == 0))
    def _():
        for t in range(2):
            pltpu.make_async_copy(
                held.at[t, pl.ds(0, half)], held.at[t, pl.ds(0, half)], send_sem.at[5 + t]
            ).wait()

    @pl.when(r == 0)
    def _():
        rows_across().wait_send()

    pltpu.make_async_copy(share, out, out_sem).wait()


def per_device(layers, front):
    height, width = front.shape
    panel = front
    if width < P_SIZE:
        parts = [front] + [
            lax.ppermute(front, ("col", "layer"), [(f, 0)]) for f in range(1, P_SIZE // width)
        ]
        panel = jnp.concatenate(parts, axis=1)
    pieces = (P_SIZE + height) // 2 // PIECE
    hbm = pl.BlockSpec(memory_space=pl.ANY)
    return pl.pallas_call(
        functools.partial(kernel, layers),
        out_shape=jax.ShapeDtypeStruct((height, width), jnp.float32),
        in_specs=[hbm, hbm],
        out_specs=hbm,
        scratch_shapes=[
            pltpu.VMEM((2, (P_SIZE + height) // 2, P_SIZE), jnp.float32),
            pltpu.VMEM((height, width), jnp.float32),
            pltpu.VMEM((P_SIZE, width), jnp.float32),
            pltpu.VMEM((P_SIZE, P_SIZE), jnp.float32),
            pltpu.VMEM((P_SIZE, P_SIZE), jnp.float32),
            pltpu.VMEM((B, B), jnp.float32),
            pltpu.VMEM((B, B), jnp.float32),
            pltpu.VMEM((P_SIZE, width), jnp.bfloat16),
            pltpu.VMEM((P_SIZE, width), jnp.bfloat16),
            pltpu.SemaphoreType.DMA((2, pieces)),
            pltpu.SemaphoreType.DMA,
            pltpu.SemaphoreType.DMA,
            pltpu.SemaphoreType.DMA,
            pltpu.SemaphoreType.DMA((8,)),
        ],
        compiler_params=pltpu.CompilerParams(
            collective_id=0, has_side_effects=True, vmem_limit_bytes=40 * 1024 * 1024
        ),
        cost_estimate=pl.CostEstimate(
            flops=6 * height * width * P_SIZE, bytes_accessed=8 * height * width, transcendentals=0
        ),
    )(front, panel)


def solution(mesh):
    placed = (P("row", ("col", "layer")),)
    return jax.shard_map(
        functools.partial(per_device, mesh.shape["layer"]),
        mesh=mesh,
        in_specs=placed,
        out_specs=P("row", ("col", "layer")),
        check_vma=False,
    )
```

```python
import functools

import jax
import jax.numpy as jnp
from jax import lax
from jax.experimental import pallas as pl
from jax.experimental.pallas import tpu as pltpu
from jax.sharding import PartitionSpec as P

B = 64
P_SIZE = 256
PIECE = 64
UNIT = 256
LEAD = 6
LAG = 8
EVERY = 2
MESH = pl.DeviceIdType.MESH


def exact_dot(left, right):
    return jnp.dot(left, right, precision=lax.Precision.HIGHEST, preferred_element_type=jnp.float32)


def split(x):
    high = x.astype(jnp.bfloat16)
    low = (x - high.astype(jnp.float32)).astype(jnp.bfloat16)
    return high, low


def fused_dot(left, right):
    return jnp.dot(left, right, preferred_element_type=jnp.float32)


def kernel(
    layers, front, panel, share,
    held, rows_in, pivot, inner, x_buf, t_buf, g_high, g_low,
    recv_sem, rows_sem, load_sem, send_sem,
):
    height, width = share.shape
    half = UNIT // 2
    pivot_pieces = P_SIZE // PIECE
    unit_pieces = half // PIECE
    units = height // UNIT
    total = pivot_pieces + units * unit_pieces
    order = list(range(pivot_pieces, pivot_pieces + LEAD)) + list(range(pivot_pieces))
    order += list(range(pivot_pieces + LEAD, total))

    r, col, z = lax.axis_index("row"), lax.axis_index("col"), lax.axis_index("layer")
    y, core = col // 2, col % 2
    flat = col * layers + z
    root_chip = jnp.logical_and(y == 0, z == 0)
    root = jnp.logical_and(root_chip, core == 0)
    has_sib = jnp.logical_not(jnp.logical_and(root_chip, core == 1))

    def device(row, yy, cc, zz):
        return (row, yy * 2 + cc, zz)

    along = jnp.logical_and(y == core, z < layers - 1)
    back = jnp.logical_and(jnp.logical_and(core == 0, y == 1), z == 1)
    has_one = jnp.logical_or(along, back)
    one = device(r, y, core, jnp.where(back, 0, jnp.minimum(z + 1, layers - 1)))
    has_two = jnp.logical_and(y == core, z >= 1)
    two = device(r, 1 - y, core, z)
    sib = device(r, y, 1 - core, z)
    tree_b = device(r, 1, 1, 0)
    other = device(1 - r, y, core, z)

    at_start = z == 0
    parent_y = jnp.where(at_start, jnp.where(core == 0, 1, 0), jnp.where(y == core, y, 1 - y))
    parent_z = jnp.where(at_start, jnp.where(core == 0, 1, 0), jnp.where(y == core, z - 1, z))
    parent_core = jnp.where(at_start, 0, core)
    barrier = pltpu.get_barrier_semaphore()

    @pl.when(jnp.logical_not(root_chip))
    def _():
        pl.semaphore_signal(
            barrier, inc=1, device_id=device(r, parent_y, parent_core, parent_z), device_id_type=MESH
        )

    @pl.when(jnp.logical_not(root))
    def _():
        pl.semaphore_signal(barrier, inc=1, device_id=sib, device_id_type=MESH)

    @pl.when(r == 1)
    def _():
        pl.semaphore_signal(barrier, inc=1, device_id=other, device_id_type=MESH)

    def row_of(t, i):
        return ((i - pivot_pieces) // unit_pieces) * UNIT + t * half + ((i - pivot_pieces) % unit_pieces) * PIECE

    @pl.when(root)
    def _():
        for i in sorted(order):
            for t in range(2):
                if i < pivot_pieces and t == 0:
                    @pl.when(r == 0)
                    def _():
                        pltpu.make_async_copy(
                            panel.at[pl.ds(i * PIECE, PIECE), pl.ds(0, P_SIZE)],
                            held.at[0, pl.ds(i * PIECE, PIECE)],
                            recv_sem.at[0, i],
                        ).start()
                elif i >= pivot_pieces:
                    pltpu.make_async_copy(
                        panel.at[pl.ds(row_of(t, i), PIECE), pl.ds(0, P_SIZE)],
                        held.at[t, pl.ds(i * PIECE, PIECE)],
                        recv_sem.at[t, i],
                    ).start()

    load = pltpu.make_async_copy(front, share, load_sem)
    load.start()

    @pl.when(r == 0)
    def _():
        pltpu.make_async_copy(front.at[pl.ds(0, P_SIZE)], rows_in, rows_sem).start()

    peers = (
        has_sib.astype(jnp.int32) + has_one.astype(jnp.int32) + has_two.astype(jnp.int32)
        + root.astype(jnp.int32) + (r == 0).astype(jnp.int32)
    )
    pl.when(peers > 0)(lambda: pl.semaphore_wait(barrier, peers))

    def piece(t, i, kind, target, source=None):
        return pltpu.make_async_remote_copy(
            src_ref=held.at[t if source is None else source, pl.ds(i * PIECE, PIECE)],
            dst_ref=held.at[t, pl.ds(i * PIECE, PIECE)],
            send_sem=send_sem.at[kind],
            recv_sem=recv_sem.at[t, i],
            device_id=target,
            device_id_type=MESH,
        )

    def arrived(t, i):
        pltpu.make_async_copy(
            held.at[t, pl.ds(i * PIECE, PIECE)], held.at[t, pl.ds(i * PIECE, PIECE)], recv_sem.at[t, i]
        ).wait()

    def forward(i):
        is_pivot = isinstance(i, int) and i < pivot_pieces
        if is_pivot:
            pl.when(jnp.logical_not(first_root))(lambda: arrived(core, i))
        else:
            arrived(core, i)

        @pl.when(has_one)
        def _():
            piece(core, i, 0, one).start()

        @pl.when(has_two)
        def _():
            piece(core, i, 1, two).start()

        if not is_pivot:
            @pl.when(has_sib)
            def _():
                piece(core, i, 2, sib).start()

        @pl.when(root)
        def _():
            if not is_pivot:
                arrived(1, i)
            piece(1, i, 3, tree_b, 0 if is_pivot else None).start()
            piece(1, i, 4, sib, 0 if is_pivot else None).start()

    first_root = jnp.logical_and(root, r == 0)

    @pl.when(first_root)
    def _():
        for i in range(pivot_pieces):
            arrived(0, i)
            piece(0, i, 5, other).start()

    def rows_across():
        return pltpu.make_async_remote_copy(
            src_ref=front.at[pl.ds(0, P_SIZE)],
            dst_ref=rows_in,
            send_sem=send_sem.at[6],
            recv_sem=rows_sem,
            device_id=other,
            device_id_type=MESH,
        )

    def other_arrived(i):
        @pl.when(jnp.logical_not(root))
        def _():
            arrived(1 - core, i)

    queue = list(order)
    stages = [0]

    def stage_done():
        stages[0] += 1
        if stages[0] % EVERY == 0:
            forward_some(1)

    def forward_some(count):
        for _ in range(min(count, len(queue))):
            forward(queue.pop(0))

    @pl.when(jnp.logical_and(r == 0, has_sib))
    def _():
        rows_across().start()

    forward_some(LEAD + pivot_pieces)

    @pl.when(jnp.logical_and(r == 0, jnp.logical_not(has_sib)))
    def _():
        rows_across().start()

    pivot[...] = held[core, pl.ds(0, P_SIZE), :]
    inner[...] = jnp.zeros_like(inner)

    eye = lax.broadcasted_iota(jnp.int32, (B, B), 0) == lax.broadcasted_iota(jnp.int32, (B, B), 1)
    blocks = P_SIZE // B
    for k in range(blocks):
        lo, hi = k * B, (k + 1) * B
        d = pivot[lo:hi, lo:hi]
        diagonal = jnp.where(eye, d, 0.0)
        down = 1.0 / jnp.sum(diagonal, axis=1, keepdims=True)
        across = 1.0 / jnp.sum(diagonal, axis=0, keepdims=True)
        x = jnp.where(eye, 2.0 * down, 0.0) - down * (d * across)
        x_buf[...] = x
        t_buf[...] = exact_dot(d, x)
        stage_done()
        x = x_buf[...]
        x = 2.0 * x - exact_dot(x, t_buf[...])
        x_buf[...] = x
        inner[lo:hi, lo:hi] = x
        stage_done()
        x = x_buf[...]
        if k < blocks - 1:
            pivot[hi:, lo:hi] = exact_dot(pivot[hi:, lo:hi], x)
            stage_done()
        if k > 0:
            inner[0:lo, lo:hi] = -exact_dot(exact_dot(inner[0:lo, 0:lo], pivot[0:lo, lo:hi]), x)
            stage_done()
        if k < blocks - 1:
            lower = pivot[hi:, lo:hi]
            pivot[hi:, hi:] = pivot[hi:, hi:] - exact_dot(lower, pivot[lo:hi, hi:])
            stage_done()

    pltpu.make_async_copy(rows_in, rows_in, rows_sem).wait()
    for k in range(blocks - 1):
        lo, hi = k * B, (k + 1) * B
        rows_in[hi:, :] = rows_in[hi:, :] - exact_dot(pivot[hi:, lo:hi], rows_in[lo:hi, :])
        stage_done()

    owned = min(width, P_SIZE)
    g = exact_dot(inner[...], rows_in[...])
    high, low = split(g)
    g_high[...] = high
    g_low[...] = low
    for f in range(P_SIZE // owned):
        @pl.when(flat == f)
        def _():
            high, low = split(-inner[:, f * owned : (f + 1) * owned])
            g_high[:, 0:owned] = high
            g_low[:, 0:owned] = low
            rows_in[:, 0:owned] = pivot[:, f * owned : (f + 1) * owned]

    load.wait()
    kept = flat * width + lax.broadcasted_iota(jnp.int32, (half, width), 1) >= P_SIZE

    def update(u):
        for j in range(unit_pieces):
            other_arrived(pivot_pieces + u * unit_pieces + j)
        start = pivot_pieces * PIECE + u * half
        if not isinstance(u, int):
            start = pl.multiple_of(start, PIECE)
        for t in range(2):
            high, low = split(held[t, pl.ds(start, half), :])
            drop = fused_dot(high, g_high[...]) + fused_dot(high, g_low[...]) + fused_dot(low, g_high[...])
            place = pl.ds(u * UNIT + t * half, half)
            share[place, :] = jnp.where(kept, share[place, :], 0.0) - drop

    @pl.when(r == 0)
    def _():
        for j in range(unit_pieces):
            other_arrived(pivot_pieces + j)
        share[0:UNIT, :] = rows_in[...]

    @pl.when(r != 0)
    def _():
        update(0)

    step_pieces = unit_pieces // 2
    forward_some(len(queue) % step_pieces)
    first = total - len(queue)
    halves = len(queue) // step_pieces
    here = 2 * units - halves
    done = 1
    behind = 0
    lag = LAG // step_pieces
    while behind < halves and done + 2 * (behind + 1) <= (here + behind + 1 - lag) // 2:
        behind += 1

    def catch_up(s, carry):
        for j in range(step_pieces):
            forward(first + s * step_pieces + j)
        update(done + 2 * s)
        update(done + 2 * s + 1)
        return carry

    lax.fori_loop(0, behind, catch_up, 0)
    first, halves, done = first + behind * step_pieces, halves - behind, done + 2 * behind

    def level(s, carry):
        for j in range(unit_pieces):
            forward(first + s * unit_pieces + j)
        update(done + s)
        return carry

    beside = min(halves // 2, units - done)
    lax.fori_loop(0, beside, level, 0)
    for i in range(first + beside * unit_pieces, total):
        forward(i)
    lax.fori_loop(done + beside, units, lambda u, c: (update(u), c)[1], 0)

    def sent(t, kind):
        pltpu.make_async_copy(held.at[t], held.at[t], send_sem.at[kind]).wait()

    pl.when(has_one)(lambda: sent(0, 0))
    pl.when(has_two)(lambda: sent(0, 1))

    @pl.when(has_sib)
    def _():
        whole = held.at[0, pl.ds(P_SIZE, height // 2)]
        pltpu.make_async_copy(whole, whole, send_sem.at[2]).wait()

    @pl.when(root)
    def _():
        sent(1, 3)
        sent(1, 4)

    @pl.when(jnp.logical_and(root, r == 0))
    def _():
        pltpu.make_async_copy(
            held.at[0, pl.ds(0, P_SIZE)], held.at[0, pl.ds(0, P_SIZE)], send_sem.at[5]
        ).wait()

    @pl.when(r == 0)
    def _():
        rows_across().wait_send()


def per_device(layers, front):
    height, width = front.shape
    panel = front
    if width < P_SIZE:
        parts = [front] + [
            lax.ppermute(front, ("col", "layer"), [(f, 0)]) for f in range(1, P_SIZE // width)
        ]
        panel = jnp.concatenate(parts, axis=1)
    pieces = (P_SIZE + height // 2) // PIECE
    hbm = pl.BlockSpec(memory_space=pl.ANY)
    return pl.pallas_call(
        functools.partial(kernel, layers),
        out_shape=jax.ShapeDtypeStruct((height, width), jnp.float32),
        in_specs=[hbm, hbm],
        out_specs=pl.BlockSpec(memory_space=pltpu.VMEM),
        scratch_shapes=[
            pltpu.VMEM((2, P_SIZE + height // 2, P_SIZE), jnp.float32),
            pltpu.VMEM((P_SIZE, width), jnp.float32),
            pltpu.VMEM((P_SIZE, P_SIZE), jnp.float32),
            pltpu.VMEM((P_SIZE, P_SIZE), jnp.float32),
            pltpu.VMEM((B, B), jnp.float32),
            pltpu.VMEM((B, B), jnp.float32),
            pltpu.VMEM((P_SIZE, width), jnp.bfloat16),
            pltpu.VMEM((P_SIZE, width), jnp.bfloat16),
            pltpu.SemaphoreType.DMA((2, pieces)),
            pltpu.SemaphoreType.DMA,
            pltpu.SemaphoreType.DMA,
            pltpu.SemaphoreType.DMA((7,)),
        ],
        compiler_params=pltpu.CompilerParams(
            collective_id=0, has_side_effects=True, vmem_limit_bytes=40 * 1024 * 1024
        ),
        cost_estimate=pl.CostEstimate(
            flops=6 * height * width * P_SIZE, bytes_accessed=8 * height * width, transcendentals=0
        ),
    )(front, panel)


def solution(mesh):
    placed = (P("row", ("col", "layer")),)
    return jax.shard_map(
        functools.partial(per_device, mesh.shape["layer"]),
        mesh=mesh,
        in_specs=placed,
        out_specs=P("row", ("col", "layer")),
        check_vma=False,
    )
```
